32 devices in a mesh: grp: 2 (over y), feat: 8 (over z, core), layer: 2 (over x), rep: 1.
Axes of the slice: x: 2, y: 2, z: 4, core: 2. Of those that a mesh axis runs over, the one named last changes fastest.
Arguments:
- pre_acts: bfloat16 [2, 1024, 8192], P('layer', 'grp', 'feat'), parts along dimension 1, may hold values from -6 to 6
- thresholds: float32 [2, 8192], P('layer', 'feat'), may hold values from 0.2 to 1.2
- tile_lists: int32 [2, 1024, 32], P('layer', 'grp'), parts along dimension 1, may hold values from 0 to 63, all different within a row
- decoders: bfloat16 [2, 1, 8192, 2048], P('layer', None, 'feat', 'rep'), may hold values from -0.1875 to 0.1875
- remainder: bfloat16 [1024, 1, 2048], P(('grp', 'feat', 'layer'), None, 'rep'), parts along dimension 0, may hold values from -6 to 6
Outputs:
- decoder_grads: bfloat16 [2, 2, 8192, 2048], P('layer', 'grp', 'feat', 'rep'), parts along dimension 1
- pre_grads: bfloat16 [2, 1024, 8192], P('layer', 'grp', ('feat', 'rep')), parts along dimension 1
The draws below stay inside these ranges and needn't reach their ends.
There are 2 independent parts, one for each index of `grp`. The reference program is written for one: setup_inputs(seed, part) draws one part's arguments, and reference() takes and returns one part's arrays. A program takes and returns all parts, laid end to end along the dimension named above; an argument that names none is the same for every part. Nothing has to cross between parts.
Inputs may be any that keep to these rules, and one draw needn't show every extreme that they name: `tile_lists`: each token names 32 different tiles of its layer.
All inputs are finite; a program needn't handle non-finite values.
Results may differ from the reference program's by a relative error of at most 0.0046.
Values may be sent and summed in bfloat16 or wider, within the bound.
A program may use at most 64 MiB of HBM per device.

```python
import jax
import jax.numpy as jnp
from jax import lax

D = 2048
TOKENS = 512
NT = 1
K = 32
LAYERS = 2
FEATURES = 8192
TILES = 64


def shard_levels(rng, dims, pieces, low, top_value):
    loudness = 1.0
    for dim, blocks in pieces:
        draws = jax.random.uniform(jax.random.fold_in(jax.random.fold_in(rng, 6), dim), (blocks,), jnp.float32, low / len(pieces), top_value / len(pieces))
        loudness = loudness * jnp.repeat(jnp.exp(draws), dims[dim] // blocks).reshape((-1,) + (1,) * (len(dims) - 1 - dim))
    return loudness


def choose_distinct(own_key, rows, number_of, top, lift):
    order = jax.random.permutation(jax.random.fold_in(own_key, 1), number_of)
    favour = order
    for power in range(3):
        favour = favour * favour // number_of
    favour = favour * lift // number_of
    chance = jax.random.randint(jax.random.fold_in(own_key, 2), (rows, number_of), 0, 4096) + favour
    fixed_rows = jax.random.permutation(jax.random.fold_in(own_key, 3), rows)[jnp.arange(number_of) % rows]
    chance = jnp.where(jnp.arange(rows)[:, None] == fixed_rows[None, :], 1 << 14, chance)
    score = chance * number_of + jnp.arange(number_of)
    return lax.top_k(score.astype(jnp.int32), top)[1].astype(jnp.int32)


def noise(own_key, shape, deviation, limit, shards=(), held_as=jnp.bfloat16):
    drawn = jax.random.normal(own_key, shape, jnp.float32) * deviation
    if len(shards) > 0:
        drawn = shard_levels(own_key, shape, shards, -0.22, 0.18) * drawn
    return jnp.clip(drawn, min=-limit, max=limit).astype(held_as)


def setup_inputs(seed: int = 0, part: int = 0) -> dict:
    splits = jax.random.split(jax.random.key(seed), 6)
    part_keys = jax.random.split(jax.random.fold_in(splits[5], part), 6)
    pre_acts = noise(part_keys[0], (LAYERS, TOKENS, FEATURES), 1.0, 6.0, ((0, 2), (2, 8)))
    thresholds = jnp.clip(0.2 + 1 * jax.random.uniform(splits[1], (LAYERS, FEATURES), jnp.float32) ** shard_levels(splits[1], (LAYERS, FEATURES), ((0, 2), (1, 8)), -0.2, 0.2), 0.2, 1.2)
    tile_lists = choose_distinct(part_keys[2], LAYERS * TOKENS, TILES, K, 8192).reshape((LAYERS, TOKENS, K))
    decoders = noise(splits[3], (LAYERS, NT, FEATURES, D), (LAYERS * FEATURES // 16) ** -0.5, 0.1875, ((0, 2), (2, 8)))
    remainder = noise(part_keys[4], (TOKENS, NT, D), 1.0, 6.0, ((0, 16),))
    return dict(pre_acts=pre_acts, thresholds=thresholds, tile_lists=tile_lists, decoders=decoders, remainder=remainder)


def layer_keep(pre_layer, theta_layer, tiles_layer):
    tile_index = jnp.arange(TILES, dtype=jnp.int32)
    hit = jnp.any(tiles_layer[:, :, None] == tile_index[None, None, :], axis=1)
    active = jnp.repeat(hit, 128, axis=1)
    return active & (pre_layer.astype(jnp.float32) > theta_layer[None, :])


def reference(pre_acts, thresholds, tile_lists, decoders, remainder):
    keeps = []
    acts = []
    for layer_one in range(LAYERS):
        keep = layer_keep(pre_acts[layer_one], thresholds[layer_one], tile_lists[layer_one])
        keeps.append(keep)
        acts.append(jnp.where(keep, pre_acts[layer_one], jnp.zeros((), jnp.bfloat16)))
    errs = []
    for target in range(NT):
        recon = jnp.zeros((TOKENS, D), jnp.float32)
        for layer_one in range(LAYERS):
            recon = recon + jnp.dot(acts[layer_one], decoders[layer_one, target], preferred_element_type=jnp.float32)
        errs.append((recon - remainder[:, target].astype(jnp.float32)).astype(jnp.bfloat16))
    dec_grads = []
    pre_grads = []
    for layer_one in range(LAYERS):
        per_target = []
        back = jnp.zeros((TOKENS, FEATURES), jnp.float32)
        for target in range(NT):
            per_target.append(jnp.dot(acts[layer_one].T, errs[target], preferred_element_type=jnp.float32).astype(jnp.bfloat16))
            back = back + jnp.dot(errs[target], decoders[layer_one, target].T, preferred_element_type=jnp.float32)
        dec_grads.append(jnp.stack(per_target, axis=0))
        pre_grads.append(jnp.where(keeps[layer_one], back, jnp.zeros((), jnp.float32)).astype(jnp.bfloat16))
    return jnp.stack(dec_grads, axis=0), jnp.stack(pre_grads, axis=0)
```

```python
import functools

import jax
import jax.numpy as jnp
from jax import lax
from jax.experimental import pallas as pl
from jax.experimental.pallas import tpu as pltpu
from jax.sharding import PartitionSpec as P

MESH = pl.DeviceIdType.MESH
F32, BF16 = jnp.float32, jnp.bfloat16


def general(pre_acts, thresholds, tile_lists, decoders, remainder):
    pre_local = pre_acts[0]
    tokens_all = pre_local.shape[0]
    feat_local = pre_local.shape[1]
    tiles_here = feat_local // 128
    first_tile = lax.axis_index("feat") * tiles_here
    tile_index = first_tile + jnp.arange(tiles_here, dtype=jnp.int32)
    hit = jnp.any(tile_lists[0][:, :, None] == tile_index[None, None, :], axis=1)
    active = jnp.broadcast_to(hit[:, :, None], (tokens_all, tiles_here, 128)).reshape(
        tokens_all, feat_local
    )
    keep = active & (pre_local.astype(F32) > thresholds[0][None, :])
    acts = jnp.where(keep, pre_local, jnp.zeros((), BF16))
    dec_local = decoders[0]
    total = lax.psum(
        jnp.einsum("tf,jfd->tjd", acts, dec_local, preferred_element_type=F32),
        ("feat", "layer"),
    )
    whole_rem = lax.all_gather(remainder, ("feat", "layer"), axis=0, tiled=True)
    error = (total - whole_rem.astype(F32)).astype(BF16)
    grad_dec = jnp.einsum("tf,tjd->jfd", acts, error, preferred_element_type=F32).astype(BF16)
    term = jnp.einsum("tjd,jfd->tf", error, dec_local, preferred_element_type=F32)
    back = lax.psum_scatter(term, "rep", scatter_dimension=1, tiled=True)
    half_width = back.shape[1]
    keep_half = lax.dynamic_slice_in_dim(keep, lax.axis_index("rep") * half_width, half_width, 1)
    grad_pre = jnp.where(keep_half, back, jnp.zeros((), F32)).astype(BF16)
    return (grad_dec[None], grad_pre[None])


def error_kernel(
    nz, nj, pre_ref, thr_ref, tiles_ref, dec_ref, rem_ref, acts_ref, err_ref,
    pf, csend, crecv, sx, xsend, xrecv, zsend, zrecv, send_sem, recv_sem,
):
    feat, x = lax.axis_index("feat"), lax.axis_index("layer")
    z, c = feat // 2, feat % 2
    width = pf.shape[-1]
    kinds = 4 + 2 * (nz - 1)
    sibling = {"feat": z * 2 + 1 - c, "layer": x}
    across = {"feat": feat, "layer": 1 - x}

    def along(k):
        return {"feat": lax.rem(z + k, nz) * 2 + c, "layer": x}

    barrier = pltpu.get_barrier_semaphore()
    for peer in [sibling, across] + [along(k) for k in range(1, nz)]:
        pl.semaphore_signal(barrier, inc=1, device_id=peer, device_id_type=MESH)

    started = []

    def send(j, kind, src, dst, peer):
        copy = pltpu.make_async_remote_copy(
            src_ref=src, dst_ref=dst, send_sem=send_sem.at[j * kinds + kind],
            recv_sem=recv_sem.at[j * kinds + kind], device_id=peer, device_id_type=MESH,
        )
        copy.start()
        started.append(copy)

    def arrived(j, kind, dst):
        pltpu.make_async_remote_copy(
            src_ref=dst, dst_ref=dst, send_sem=send_sem.at[j * kinds + kind],
            recv_sem=recv_sem.at[j * kinds + kind], device_id=sibling, device_id_type=MESH,
        ).wait_recv()

    tiles_here = pre_ref.shape[1] // 128
    listed = tiles_ref[...]
    for i in range(tiles_here):
        cols = slice(i * 128, (i + 1) * 128)
        hit = jnp.max(
            jnp.where(listed == feat * tiles_here + i, 1.0, 0.0), axis=1, keepdims=True
        )
        pre = pre_ref[:, cols].astype(F32)
        keep = jnp.where(pre > thr_ref[:, cols], hit, 0.0) > 0.0
        acts_ref[:, cols] = jnp.where(keep, pre, 0.0).astype(BF16)

    def multiply(j):
        part = jnp.dot(
            acts_ref[...], dec_ref[:, j * width:(j + 1) * width], preferred_element_type=F32
        )
        pf[j] = part.reshape(pf.shape[1:])
        csend[j] = pf[j, :, 1 - c].astype(BF16)
        if j == 0:
            pl.semaphore_wait(barrier, nz + 1)
        send(j, 0, csend.at[j], crecv.at[j], sibling)

    def add_core(j):
        arrived(j, 0, crecv.at[j])
        xsend[j] = (pf[j, :, c, 1 - x] + crecv[j, :, 1 - x].astype(F32)).astype(BF16)
        send(j, 1, xsend.at[j], xrecv.at[j], across)
        sx[j] = pf[j, :, c, x] + crecv[j, :, x].astype(F32)

    def add_layer(j):
        arrived(j, 1, xrecv.at[j])
        both = sx[j] + xrecv[j].astype(F32)
        sx[j] = both
        zsend[j] = both.astype(BF16)
        for k in range(1, nz):
            send(j, 3 + k, zsend.at[j, lax.rem(z + k, nz)], zrecv.at[j, k - 1], along(k))

    def finish(j):
        total = sx[j, z]
        for k in range(1, nz):
            arrived(j, 3 + k, zrecv.at[j, k - 1])
            total = total + zrecv[j, k - 1].astype(F32)
        rem = rem_ref[:, j * width:(j + 1) * width].astype(F32)
        err_ref[j, z, c, x] = (total - rem).astype(BF16)
        own = err_ref.at[j, z, c, x]
        for k in range(1, nz):
            send(j, 2 + nz + k, own, own, along(k))

    def spread_layer(j):
        for k in range(1, nz):
            arrived(j, 2 + nz + k, err_ref.at[j, lax.rem(z + nz - k, nz), c, x])
        send(j, 2, err_ref.at[j, :, c, x], err_ref.at[j, :, c, x], across)

    def spread_core(j):
        arrived(j, 2, err_ref.at[j, :, c, 1 - x])
        send(j, 3, err_ref.at[j, :, c], err_ref.at[j, :, c], sibling)

    def whole(j):
        arrived(j, 3, err_ref.at[j, :, 1 - c])

    stages = [(multiply, 0), (add_core, 1), (add_layer, 4), (finish, 6), (spread_layer, 8),
              (spread_core, 10), (whole, 12)]
    for now in range(nj + 12):
        for stage, after in stages:
            if 0 <= now - after < nj:
                stage(now - after)
    for copy in started:
        copy.wait_send()


def grads_kernel(acts_ref, err_ref, dec_ref, gd_ref, gp_ref):
    nj, _, width = err_ref.shape
    acts = acts_ref[...]
    back = jnp.zeros(gp_ref.shape, F32)
    for j in range(nj):
        cols = slice(j * width, (j + 1) * width)
        err = err_ref[j]
        gd_ref[:, cols] = lax.dot_general(
            acts, err, (((0,), (0,)), ((), ())), preferred_element_type=F32
        ).astype(BF16)
        back += lax.dot_general(
            err, dec_ref[:, cols], (((1,), (1,)), ((), ())), preferred_element_type=F32
        )
    gp_ref[...] = jnp.where(acts.astype(F32) > 0.0, back, 0.0).astype(BF16)


def staged(nz, nj, pre_acts, thresholds, tile_lists, decoders, remainder):
    _, tokens, features = pre_acts.shape
    model = decoders.shape[3]
    width, rows = model // nj, remainder.shape[0]
    kinds = nj * (4 + 2 * (nz - 1))
    vmem = pl.BlockSpec(memory_space=pltpu.VMEM)
    dec = decoders.reshape(features, model)
    acts, err = pl.pallas_call(
        functools.partial(error_kernel, nz, nj),
        out_shape=(
            jax.ShapeDtypeStruct((tokens, features), BF16),
            jax.ShapeDtypeStruct((nj, nz, 2, 2, rows, width), BF16),
        ),
        in_specs=[vmem] * 5,
        out_specs=(vmem, vmem),
        scratch_shapes=[
            pltpu.VMEM((nj, nz, 2, 2, rows, width), F32),
            pltpu.VMEM((nj, nz, 2, rows, width), BF16),
            pltpu.VMEM((nj, nz, 2, rows, width), BF16),
            pltpu.VMEM((nj, nz, rows, width), F32),
            pltpu.VMEM((nj, nz, rows, width), BF16),
            pltpu.VMEM((nj, nz, rows, width), BF16),
            pltpu.VMEM((nj, nz, rows, width), BF16),
            pltpu.VMEM((nj, nz - 1, rows, width), BF16),
            pltpu.SemaphoreType.DMA((kinds,)),
            pltpu.SemaphoreType.DMA((kinds,)),
        ],
        compiler_params=pltpu.CompilerParams(
            collective_id=0, has_side_effects=True, vmem_limit_bytes=40 << 20
        ),
        cost_estimate=pl.CostEstimate(
            flops=2 * tokens * features * model, bytes_accessed=12 << 20, transcendentals=0
        ),
    )(
        pre_acts.reshape(tokens, features), thresholds, tile_lists.reshape(tokens, -1), dec,
        remainder.reshape(rows, model),
    )
    block = 256
    grad_dec, grad_pre = pl.pallas_call(
        grads_kernel,
        grid=(features // block,),
        out_shape=(
            jax.ShapeDtypeStruct((features, model), BF16),
            jax.ShapeDtypeStruct((tokens, features), BF16),
        ),
        in_specs=[
            pl.BlockSpec((tokens, block), lambda i: (0, i)),
            pl.BlockSpec((nj, tokens, width), lambda i: (0, 0, 0)),
            pl.BlockSpec((block, model), lambda i: (i, 0)),
        ],
        out_specs=(
            pl.BlockSpec((block, model), lambda i: (i, 0)),
            pl.BlockSpec((tokens, block), lambda i: (0, i)),
        ),
        compiler_params=pltpu.CompilerParams(vmem_limit_bytes=32 << 20),
        cost_estimate=pl.CostEstimate(
            flops=4 * tokens * features * model, bytes_accessed=14 << 20, transcendentals=0
        ),
    )(acts, err.reshape(nj, tokens, width), dec)
    return grad_dec[None, None], grad_pre[None]


def solution(mesh):
    in_specs = (
        P("layer", "grp", "feat"),
        P("layer", "feat"),
        P("layer", "grp", None),
        P("layer", None, "feat", "rep"),
        P(("grp", "feat", "layer"), None, "rep"),
    )
    out_specs = (P("layer", "grp", "feat", "rep"), P("layer", "grp", ("feat", "rep")))

    def shards(*args):
        feat, layer = mesh.shape["feat"], mesh.shape["layer"]
        rows = args[4].shape[0]
        pairs = feat % 2 == 0 and feat >= 4 and layer == 2 and mesh.shape["rep"] == 1
        if pairs and rows % 16 == 0 and args[3].shape[1] == 1:
            return staged(feat // 2, 4, *args)
        return general(*args)

    return jax.shard_map(shards, mesh=mesh, in_specs=in_specs, out_specs=out_specs, check_vma=False)
```

```python
import functools

import jax
import jax.numpy as jnp
from jax import lax
from jax.experimental import pallas as pl
from jax.experimental.pallas import tpu as pltpu
from jax.sharding import PartitionSpec as P

MESH = pl.DeviceIdType.MESH
F32, BF16 = jnp.float32, jnp.bfloat16


def general(pre_acts, thresholds, tile_lists, decoders, remainder):
    pre_local = pre_acts[0]
    tokens_all = pre_local.shape[0]
    feat_local = pre_local.shape[1]
    tiles_here = feat_local // 128
    first_tile = lax.axis_index("feat") * tiles_here
    tile_index = first_tile + jnp.arange(tiles_here, dtype=jnp.int32)
    hit = jnp.any(tile_lists[0][:, :, None] == tile_index[None, None, :], axis=1)
    active = jnp.broadcast_to(hit[:, :, None], (tokens_all, tiles_here, 128)).reshape(
        tokens_all, feat_local
    )
    keep = active & (pre_local.astype(F32) > thresholds[0][None, :])
    acts = jnp.where(keep, pre_local, jnp.zeros((), BF16))
    dec_local = decoders[0]
    total = lax.psum(
        jnp.einsum("tf,jfd->tjd", acts, dec_local, preferred_element_type=F32),
        ("feat", "layer"),
    )
    whole_rem = lax.all_gather(remainder, ("feat", "layer"), axis=0, tiled=True)
    error = (total - whole_rem.astype(F32)).astype(BF16)
    grad_dec = jnp.einsum("tf,tjd->jfd", acts, error, preferred_element_type=F32).astype(BF16)
    term = jnp.einsum("tjd,jfd->tf", error, dec_local, preferred_element_type=F32)
    back = lax.psum_scatter(term, "rep", scatter_dimension=1, tiled=True)
    half_width = back.shape[1]
    keep_half = lax.dynamic_slice_in_dim(keep, lax.axis_index("rep") * half_width, half_width, 1)
    grad_pre = jnp.where(keep_half, back, jnp.zeros((), F32)).astype(BF16)
    return (grad_dec[None], grad_pre[None])


def window_kernel(
    nj, pre_hbm, thr_hbm, tiles_hbm, dec_hbm, rem_hbm, gd_ref, gp_ref,
    pre_ref, thr_ref, tiles_ref, dec_ref, rem_ref, acts_ref, flipped, back, err_ref,
    pf, csend, crecv, sx, xsend, xrecv, psend, precv, msend, mrecv,
    send_sem, recv_sem, load_sem,
):
    feat, x = lax.axis_index("feat"), lax.axis_index("layer")
    c = feat % 2
    zl, zh = feat // 2 % 2, feat // 4
    width = pf.shape[-1]
    features = pre_ref.shape[1]
    sibling = {"feat": feat + 1 - 2 * c, "layer": x}
    across = {"feat": feat, "layer": 1 - x}
    beside = {"feat": feat + 2 - 4 * zl, "layer": x}
    beyond = {"feat": feat + 4 - 8 * zh, "layer": x}

    barrier = pltpu.get_barrier_semaphore()
    for peer in (sibling, across, beside, beyond):
        pl.semaphore_signal(barrier, inc=1, device_id=peer, device_id_type=MESH)

    def cols(j):
        return slice(j * width, (j + 1) * width)

    loads = [
        pltpu.make_async_copy(src, dst, load_sem.at[i])
        for i, (src, dst) in enumerate(
            [(tiles_hbm, tiles_ref), (thr_hbm, thr_ref), (pre_hbm, pre_ref)]
            + [(dec_hbm.at[:, cols(j)], dec_ref.at[:, cols(j)]) for j in range(nj)]
            + [(rem_hbm, rem_ref)]
        )
    ]
    for load in loads:
        load.start()

    started = []

    def send(j, kind, src, dst, peer):
        copy = pltpu.make_async_remote_copy(
            src_ref=src, dst_ref=dst, send_sem=send_sem.at[j * 8 + kind],
            recv_sem=recv_sem.at[j * 8 + kind], device_id=peer, device_id_type=MESH,
        )
        copy.start()
        started.append(copy)

    def arrived(j, kind, dst):
        pltpu.make_async_remote_copy(
            src_ref=dst, dst_ref=dst, send_sem=send_sem.at[j * 8 + kind],
            recv_sem=recv_sem.at[j * 8 + kind], device_id=sibling, device_id_type=MESH,
        ).wait_recv()

    tiles_here = features // 128
    loads[0].wait()
    listed = tiles_ref[...]
    named = jnp.concatenate(
        [jnp.where(listed == feat * tiles_here + i, 1.0, 0.0) for i in range(tiles_here)], axis=0
    ).astype(BF16)
    shape = (named.shape[0], features)
    row_tile = lax.broadcasted_iota(jnp.int32, shape, 0) // listed.shape[0]
    col_tile = lax.broadcasted_iota(jnp.int32, shape, 1) // 128
    spread = jnp.where(row_tile == col_tile, 1.0, 0.0).astype(BF16)
    loads[1].wait()
    loads[2].wait()
    for i in range(0, features, 256):
        part = slice(i, i + 256)
        hit = lax.dot_general(
            named, spread[:, part], (((0,), (0,)), ((), ())), preferred_element_type=F32
        )
        pre = pre_ref[:, part].astype(F32)
        keep = jnp.where(pre > thr_ref[:, part], hit, 0.0) > 0.0
        acts_ref[:, part] = jnp.where(keep, pre, 0.0).astype(BF16)

    def multiply(j):
        loads[3 + j].wait()
        part = jnp.dot(acts_ref[...], dec_ref[:, cols(j)], preferred_element_type=F32)
        pf[j] = part.reshape(pf.shape[1:])
        csend[j] = pf[j, :, :, 1 - c].astype(BF16)
        if j == 0:
            pl.semaphore_wait(barrier, 4)
        send(j, 0, csend.at[j], crecv.at[j], sibling)
        if j == 0:
            loads[3 + nj].wait()

    def add_core(j):
        arrived(j, 0, crecv.at[j])
        xsend[j] = (pf[j, :, :, c, 1 - x] + crecv[j, :, :, 1 - x].astype(F32)).astype(BF16)
        send(j, 1, xsend.at[j], xrecv.at[j], across)
        sx[j] = pf[j, :, :, c, x] + crecv[j, :, :, x].astype(F32)

    def add_layer(j):
        arrived(j, 1, xrecv.at[j])
        psend[j] = (sx[j, :, 1 - zl] + xrecv[j, :, 1 - zl].astype(F32)).astype(BF16)
        send(j, 2, psend.at[j], precv.at[j], beside)

    def add_beside(j):
        arrived(j, 2, precv.at[j])
        far = sx[j, 1 - zh, zl] + xrecv[j, 1 - zh, zl].astype(F32)
        msend[j] = (far + precv[j, 1 - zh].astype(F32)).astype(BF16)
        send(j, 3, msend.at[j], mrecv.at[j], beyond)

    def finish(j):
        near = sx[j, zh, zl] + xrecv[j, zh, zl].astype(F32) + precv[j, zh].astype(F32)
        rem = rem_ref[:, cols(j)].astype(F32)
        arrived(j, 3, mrecv.at[j])
        err_ref[j, zh, zl, c, x] = (near + mrecv[j].astype(F32) - rem).astype(BF16)
        own = err_ref.at[j, zh, zl, c, x]
        send(j, 4, own, own, beyond)

    def pass_beside(j):
        arrived(j, 4, err_ref.at[j, 1 - zh, zl, c, x])
        send(j, 5, err_ref.at[j, :, zl, c, x], err_ref.at[j, :, zl, c, x], beside)

    def pass_across(j):
        arrived(j, 5, err_ref.at[j, :, 1 - zl, c, x])
        send(j, 6, err_ref.at[j, :, :, c, x], err_ref.at[j, :, :, c, x], across)

    def pass_sibling(j):
        arrived(j, 6, err_ref.at[j, :, :, c, 1 - x])
        send(j, 7, err_ref.at[j, :, :, c], err_ref.at[j, :, :, c], sibling)

    def gradients(j):
        arrived(j, 7, err_ref.at[j, :, :, 1 - c])
        err = err_ref[j].reshape(acts_ref.shape[0], width)
        gd_ref[:, cols(j)] = jnp.dot(
            flipped[...], err, preferred_element_type=F32
        ).astype(BF16)
        term = lax.dot_general(
            err, dec_ref[:, cols(j)], (((1,), (1,)), ((), ())), preferred_element_type=F32
        )
        if j == 0:
            back[...] = term
        elif j < nj - 1:
            back[...] += term
        else:
            term = back[...] + term
            gp_ref[...] = jnp.where(acts_ref[...].astype(F32) > 0.0, term, 0.0).astype(BF16)

    def flip(j):
        if j == nj - 1:
            for i in range(0, features, 128):
                flipped[i:i + 128, :] = acts_ref[:, i:i + 128].T

    stages = [(multiply, 0), (add_core, 1), (add_layer, 3), (add_beside, 5), (finish, 7),
              (pass_beside, 9), (pass_across, 11), (pass_sibling, 13), (flip, 1), (gradients, 14)]
    for now in range(nj + max(after for _, after in stages)):
        for stage, after in stages:
            if 0 <= now - after < nj:
                stage(now - after)
    for copy in started:
        copy.wait_send()


def staged(nj, pre_acts, thresholds, tile_lists, decoders, remainder):
    _, tokens, features = pre_acts.shape
    model, listed = decoders.shape[3], tile_lists.shape[2]
    width, rows = model // nj, remainder.shape[0]
    hbm = pl.BlockSpec(memory_space=pltpu.HBM)
    vmem = pl.BlockSpec(memory_space=pltpu.VMEM)
    grad_dec, grad_pre = pl.pallas_call(
        functools.partial(window_kernel, nj),
        out_shape=(
            jax.ShapeDtypeStruct((features, model), BF16),
            jax.ShapeDtypeStruct((tokens, features), BF16),
        ),
        in_specs=[hbm] * 5,
        out_specs=(vmem, vmem),
        scratch_shapes=[
            pltpu.VMEM((tokens, features), BF16),
            pltpu.VMEM((1, features), F32),
            pltpu.VMEM((listed, tokens), jnp.int32),
            pltpu.VMEM((features, model), BF16),
            pltpu.VMEM((rows, model), BF16),
            pltpu.VMEM((tokens, features), BF16),
            pltpu.VMEM((features, tokens), BF16),
            pltpu.VMEM((tokens, features), F32),
            pltpu.VMEM((nj, 2, 2, 2, 2, rows, width), BF16),
            pltpu.VMEM((nj, 2, 2, 2, 2, rows, width), F32),
            pltpu.VMEM((nj, 2, 2, 2, rows, width), BF16),
            pltpu.VMEM((nj, 2, 2, 2, rows, width), BF16),
            pltpu.VMEM((nj, 2, 2, rows, width), F32),
            pltpu.VMEM((nj, 2, 2, rows, width), BF16),
            pltpu.VMEM((nj, 2, 2, rows, width), BF16),
            pltpu.VMEM((nj, 2, rows, width), BF16),
            pltpu.VMEM((nj, 2, rows, width), BF16),
            pltpu.VMEM((nj, rows, width), BF16),
            pltpu.VMEM((nj, rows, width), BF16),
            pltpu.SemaphoreType.DMA((nj * 8,)),
            pltpu.SemaphoreType.DMA((nj * 8,)),
            pltpu.SemaphoreType.DMA((nj + 4,)),
        ],
        compiler_params=pltpu.CompilerParams(
            collective_id=0, has_side_effects=True, vmem_limit_bytes=44 << 20
        ),
        cost_estimate=pl.CostEstimate(
            flops=6 * tokens * features * model, bytes_accessed=12 << 20, transcendentals=0
        ),
    )(
        pre_acts.reshape(tokens, features), thresholds, tile_lists.reshape(tokens, listed).T,
        decoders.reshape(features, model), remainder.reshape(rows, model),
    )
    return grad_dec[None, None], grad_pre[None]


def solution(mesh):
    in_specs = (
        P("layer", "grp", "feat"),
        P("layer", "feat"),
        P("layer", "grp", None),
        P("layer", None, "feat", "rep"),
        P(("grp", "feat", "layer"), None, "rep"),
    )
    out_specs = (P("layer", "grp", "feat", "rep"), P("layer", "grp", ("feat", "rep")))

    def shards(*args):
        feat, layer = mesh.shape["feat"], mesh.shape["layer"]
        rows = args[4].shape[0]
        halved = feat == 8 and layer == 2 and mesh.shape["rep"] == 1
        if halved and rows % 16 == 0 and args[3].shape[1] == 1:
            return staged(8, *args)
        return general(*args)

    return jax.shard_map(shards, mesh=mesh, in_specs=in_specs, out_specs=out_specs, check_vma=False)
```

```python
import functools

import jax
import jax.numpy as jnp
from jax import lax
from jax.experimental import pallas as pl
from jax.experimental.pallas import tpu as pltpu
from jax.sharding import PartitionSpec as P

MESH = pl.DeviceIdType.MESH
F32, BF16 = jnp.float32, jnp.bfloat16


def general(pre_acts, thresholds, tile_lists, decoders, remainder):
    pre_local = pre_acts[0]
    tokens_all = pre_local.shape[0]
    feat_local = pre_local.shape[1]
    tiles_here = feat_local // 128
    first_tile = lax.axis_index("feat") * tiles_here
    tile_index = first_tile + jnp.arange(tiles_here, dtype=jnp.int32)
    hit = jnp.any(tile_lists[0][:, :, None] == tile_index[None, None, :], axis=1)
    active = jnp.broadcast_to(hit[:, :, None], (tokens_all, tiles_here, 128)).reshape(
        tokens_all, feat_local
    )
    keep = active & (pre_local.astype(F32) > thresholds[0][None, :])
    acts = jnp.where(keep, pre_local, jnp.zeros((), BF16))
    dec_local = decoders[0]
    total = lax.psum(
        jnp.einsum("tf,jfd->tjd", acts, dec_local, preferred_element_type=F32),
        ("feat", "layer"),
    )
    whole_rem = lax.all_gather(remainder, ("feat", "layer"), axis=0, tiled=True)
    error = (total - whole_rem.astype(F32)).astype(BF16)
    grad_dec = jnp.einsum("tf,tjd->jfd", acts, error, preferred_element_type=F32).astype(BF16)
    term = jnp.einsum("tjd,jfd->tf", error, dec_local, preferred_element_type=F32)
    back = lax.psum_scatter(term, "rep", scatter_dimension=1, tiled=True)
    half_width = back.shape[1]
    keep_half = lax.dynamic_slice_in_dim(keep, lax.axis_index("rep") * half_width, half_width, 1)
    grad_pre = jnp.where(keep_half, back, jnp.zeros((), F32)).astype(BF16)
    return (grad_dec[None], grad_pre[None])


def window_kernel(
    nj, pre_hbm, thr_hbm, tiles_hbm, dec_hbm, rem_hbm, gd_ref, gp_ref,
    pre_ref, thr_ref, tiles_ref, dec_ref, rem_ref, acts_ref, flipped, back, err_ref,
    pf, csend, crecv, sx, xsend, xrecv, psend, precv, msend, mrecv,
    send_sem, recv_sem, load_sem,
):
    feat, x = lax.axis_index("feat"), lax.axis_index("layer")
    c = feat % 2
    zl, zh = feat // 2 % 2, feat // 4
    width = pf.shape[-1]
    features = pre_ref.shape[1]
    sibling = {"feat": feat + 1 - 2 * c, "layer": x}
    across = {"feat": feat, "layer": 1 - x}
    beside = {"feat": feat + 2 - 4 * zl, "layer": x}
    beyond = {"feat": feat + 4 - 8 * zh, "layer": x}
    corner = {"feat": feat + 6 - 4 * zl - 8 * zh, "layer": x}

    barrier = pltpu.get_barrier_semaphore()
    for peer in (sibling, across, beside, beyond, corner):
        pl.semaphore_signal(barrier, inc=1, device_id=peer, device_id_type=MESH)

    def cols(j):
        return slice(j * width, (j + 1) * width)

    loads = [
        pltpu.make_async_copy(src, dst, load_sem.at[i])
        for i, (src, dst) in enumerate(
            [(tiles_hbm, tiles_ref), (thr_hbm, thr_ref), (pre_hbm, pre_ref)]
            + [(dec_hbm.at[:, cols(j)], dec_ref.at[:, cols(j)]) for j in range(nj)]
            + [(rem_hbm, rem_ref)]
        )
    ]
    for load in loads:
        load.start()

    started = []

    def send(j, kind, src, dst, peer):
        copy = pltpu.make_async_remote_copy(
            src_ref=src, dst_ref=dst, send_sem=send_sem.at[j * 9 + kind],
            recv_sem=recv_sem.at[j * 9 + kind], device_id=peer, device_id_type=MESH,
        )
        copy.start()
        started.append(copy)

    def arrived(j, kind, dst):
        pltpu.make_async_remote_copy(
            src_ref=dst, dst_ref=dst, send_sem=send_sem.at[j * 9 + kind],
            recv_sem=recv_sem.at[j * 9 + kind], device_id=sibling, device_id_type=MESH,
        ).wait_recv()

    tiles_here = features // 128
    listed_count = tiles_ref.shape[0]
    shape = (listed_count * tiles_here, features)
    row_tile = lax.broadcasted_iota(jnp.int32, shape, 0) // listed_count
    col_tile = lax.broadcasted_iota(jnp.int32, shape, 1) // 128
    spread = jnp.where(row_tile == col_tile, 1.0, 0.0).astype(BF16)
    loads[0].wait()
    listed = tiles_ref[...]
    named = jnp.concatenate(
        [jnp.where(listed == feat * tiles_here + i, 1.0, 0.0) for i in range(tiles_here)], axis=0
    ).astype(BF16)
    loads[1].wait()
    loads[2].wait()
    for i in range(0, features, 256):
        part = slice(i, i + 256)
        hit = lax.dot_general(
            named, spread[:, part], (((0,), (0,)), ((), ())), preferred_element_type=F32
        )
        pre = pre_ref[:, part].astype(F32)
        keep = jnp.where(pre > thr_ref[:, part], hit, 0.0) > 0.0
        acts_ref[:, part] = jnp.where(keep, pre, 0.0).astype(BF16)

    def multiply(j):
        loads[3 + j].wait()
        part = jnp.dot(acts_ref[...], dec_ref[:, cols(j)], preferred_element_type=F32)
        pf[j] = part.reshape(pf.shape[1:])
        csend[j] = pf[j, :, :, 1 - c].astype(BF16)
        if j == 0:
            pl.semaphore_wait(barrier, 5)
        send(j, 0, csend.at[j], crecv.at[j], sibling)
        if j == 0:
            loads[3 + nj].wait()

    def add_core(j):
        arrived(j, 0, crecv.at[j])
        xsend[j] = (pf[j, :, :, c, 1 - x] + crecv[j, :, :, 1 - x].astype(F32)).astype(BF16)
        send(j, 1, xsend.at[j], xrecv.at[j], across)
        sx[j] = pf[j, :, :, c, x] + crecv[j, :, :, x].astype(F32)

    def add_layer(j):
        arrived(j, 1, xrecv.at[j])
        psend[j] = (sx[j, :, 1 - zl] + xrecv[j, :, 1 - zl].astype(F32)).astype(BF16)
        send(j, 2, psend.at[j], precv.at[j], beside)

    def add_beside(j):
        arrived(j, 2, precv.at[j])
        far = sx[j, 1 - zh, zl] + xrecv[j, 1 - zh, zl].astype(F32)
        msend[j] = (far + precv[j, 1 - zh].astype(F32)).astype(BF16)
        send(j, 3, msend.at[j], mrecv.at[j], beyond)

    def finish(j):
        near = sx[j, zh, zl] + xrecv[j, zh, zl].astype(F32) + precv[j, zh].astype(F32)
        rem = rem_ref[:, cols(j)].astype(F32)
        arrived(j, 3, mrecv.at[j])
        err_ref[j, zh, zl, c, x] = (near + mrecv[j].astype(F32) - rem).astype(BF16)
        own = err_ref.at[j, zh, zl, c, x]
        send(j, 4, own, own, beyond)
        send(j, 5, own, own, corner)
        send(j, 6, own, own, beside)

    def pass_across(j):
        arrived(j, 4, err_ref.at[j, 1 - zh, zl, c, x])
        arrived(j, 5, err_ref.at[j, 1 - zh, 1 - zl, c, x])
        arrived(j, 6, err_ref.at[j, zh, 1 - zl, c, x])
        send(j, 7, err_ref.at[j, :, :, c, x], err_ref.at[j, :, :, c, x], across)

    def pass_sibling(j):
        arrived(j, 7, err_ref.at[j, :, :, c, 1 - x])
        send(j, 8, err_ref.at[j, :, :, c], err_ref.at[j, :, :, c], sibling)

    def gradients(j):
        arrived(j, 8, err_ref.at[j, :, :, 1 - c])
        err = err_ref[j].reshape(acts_ref.shape[0], width)
        gd_ref[:, cols(j)] = jnp.dot(
            flipped[...], err, preferred_element_type=F32
        ).astype(BF16)
        term = lax.dot_general(
            err, dec_ref[:, cols(j)], (((1,), (1,)), ((), ())), preferred_element_type=F32
        )
        if j == 0:
            back[...] = term
        elif j < nj - 1:
            back[...] += term
        else:
            term = back[...] + term
            gp_ref[...] = jnp.where(acts_ref[...].astype(F32) > 0.0, term, 0.0).astype(BF16)

    def flip(j):
        if j == nj - 1:
            for i in range(0, features, 128):
                flipped[i:i + 128, :] = acts_ref[:, i:i + 128].T

    stages = [(multiply, 0), (add_core, 1), (add_layer, 3), (add_beside, 5), (finish, 7), (pass_across, 9), (pass_sibling, 11), (gradients, 12), (flip, 1)]
    for now in range(nj + max(after for _, after in stages)):
        for stage, after in stages:
            if 0 <= now - after < nj:
                stage(now - after)
    for copy in started:
        copy.wait_send()


def store_kernel(gd_ref, gp_ref, gd_hbm, gp_hbm, sem):
    rows = gd_ref.shape[0] // 4
    copies = [
        pltpu.make_async_copy(gd_ref.at[i * rows:(i + 1) * rows], gd_hbm.at[i * rows:(i + 1) * rows], sem.at[i])
        for i in range(4)
    ] + [pltpu.make_async_copy(gp_ref, gp_hbm, sem.at[4])]
    for copy in copies:
        copy.start()
    for copy in copies:
        copy.wait()


def staged(nj, pre_acts, thresholds, tile_lists, decoders, remainder):
    _, tokens, features = pre_acts.shape
    model, listed = decoders.shape[3], tile_lists.shape[2]
    width, rows = model // nj, remainder.shape[0]
    hbm = pl.BlockSpec(memory_space=pltpu.HBM)
    vmem = pl.BlockSpec(memory_space=pltpu.VMEM)
    grad_dec, grad_pre = pl.pallas_call(
        functools.partial(window_kernel, nj),
        out_shape=(
            jax.ShapeDtypeStruct((features, model), BF16),
            jax.ShapeDtypeStruct((tokens, features), BF16),
        ),
        in_specs=[hbm] * 5,
        out_specs=(vmem, vmem),
        scratch_shapes=[
            pltpu.VMEM((tokens, features), BF16),
            pltpu.VMEM((1, features), F32),
            pltpu.VMEM((listed, tokens), jnp.int32),
            pltpu.VMEM((features, model), BF16),
            pltpu.VMEM((rows, model), BF16),
            pltpu.VMEM((tokens, features), BF16),
            pltpu.VMEM((features, tokens), BF16),
            pltpu.VMEM((tokens, features), F32),
            pltpu.VMEM((nj, 2, 2, 2, 2, rows, width), BF16),
            pltpu.VMEM((nj, 2, 2, 2, 2, rows, width), F32),
            pltpu.VMEM((nj, 2, 2, 2, rows, width), BF16),
            pltpu.VMEM((nj, 2, 2, 2, rows, width), BF16),
            pltpu.VMEM((nj, 2, 2, rows, width), F32),
            pltpu.VMEM((nj, 2, 2, rows, width), BF16),
            pltpu.VMEM((nj, 2, 2, rows, width), BF16),
            pltpu.VMEM((nj, 2, rows, width), BF16),
            pltpu.VMEM((nj, 2, rows, width), BF16),
            pltpu.VMEM((nj, rows, width), BF16),
            pltpu.VMEM((nj, rows, width), BF16),
            pltpu.SemaphoreType.DMA((nj * 9,)),
            pltpu.SemaphoreType.DMA((nj * 9,)),
            pltpu.SemaphoreType.DMA((nj + 4,)),
        ],
        compiler_params=pltpu.CompilerParams(
            collective_id=0, has_side_effects=True, vmem_limit_bytes=46137344
        ),
        cost_estimate=pl.CostEstimate(
            flops=6 * tokens * features * model, bytes_accessed=12 << 20, transcendentals=0
        ),
    )(
        *(
            pltpu.with_memory_space_constraint(array, pltpu.HBM)
            for array in (
                pre_acts.reshape(tokens, features), thresholds, tile_lists.reshape(tokens, listed).T,
                decoders.reshape(features, model), remainder.reshape(rows, model),
            )
        )
    )
    grad_dec, grad_pre = pl.pallas_call(
        store_kernel,
        out_shape=(
            jax.ShapeDtypeStruct((features, model), BF16),
            jax.ShapeDtypeStruct((tokens, features), BF16),
        ),
        in_specs=[pl.BlockSpec(memory_space=pl.ANY)] * 2,
        out_specs=(hbm, hbm),
        scratch_shapes=[pltpu.SemaphoreType.DMA((5,))],
        compiler_params=pltpu.CompilerParams(vmem_limit_bytes=1 << 20),
    )(grad_dec, grad_pre)
    return grad_dec[None, None], grad_pre[None]


def solution(mesh):
    in_specs = (
        P("layer", "grp", "feat"),
        P("layer", "feat"),
        P("layer", "grp", None),
        P("layer", None, "feat", "rep"),
        P(("grp", "feat", "layer"), None, "rep"),
    )
    out_specs = (P("layer", "grp", "feat", "rep"), P("layer", "grp", ("feat", "rep")))

    def shards(*args):
        feat, layer = mesh.shape["feat"], mesh.shape["layer"]
        rows = args[4].shape[0]
        halved = feat == 8 and layer == 2 and mesh.shape["rep"] == 1
        if halved and rows % 16 == 0 and args[3].shape[1] == 1:
            return staged(8, *args)
        return general(*args)

    return jax.shard_map(shards, mesh=mesh, in_specs=in_specs, out_specs=out_specs, check_vma=False)
```

```python
import functools

import jax
import jax.numpy as jnp
from jax import lax
from jax.experimental import pallas as pl
from jax.experimental.pallas import tpu as pltpu
from jax.sharding import PartitionSpec as P

MESH = pl.DeviceIdType.MESH
F32, BF16 = jnp.float32, jnp.bfloat16


def general(pre_acts, thresholds, tile_lists, decoders, remainder):
    pre_local = pre_acts[0]
    tokens_all = pre_local.shape[0]
    feat_local = pre_local.shape[1]
    tiles_here = feat_local // 128
    first_tile = lax.axis_index("feat") * tiles_here
    tile_index = first_tile + jnp.arange(tiles_here, dtype=jnp.int32)
    hit = jnp.any(tile_lists[0][:, :, None] == tile_index[None, None, :], axis=1)
    active = jnp.broadcast_to(hit[:, :, None], (tokens_all, tiles_here, 128)).reshape(
        tokens_all, feat_local
    )
    keep = active & (pre_local.astype(F32) > thresholds[0][None, :])
    acts = jnp.where(keep, pre_local, jnp.zeros((), BF16))
    dec_local = decoders[0]
    total = lax.psum(
        jnp.einsum("tf,jfd->tjd", acts, dec_local, preferred_element_type=F32),
        ("feat", "layer"),
    )
    whole_rem = lax.all_gather(remainder, ("feat", "layer"), axis=0, tiled=True)
    error = (total - whole_rem.astype(F32)).astype(BF16)
    grad_dec = jnp.einsum("tf,tjd->jfd", acts, error, preferred_element_type=F32).astype(BF16)
    term = jnp.einsum("tjd,jfd->tf", error, dec_local, preferred_element_type=F32)
    back = lax.psum_scatter(term, "rep", scatter_dimension=1, tiled=True)
    half_width = back.shape[1]
    keep_half = lax.dynamic_slice_in_dim(keep, lax.axis_index("rep") * half_width, half_width, 1)
    grad_pre = jnp.where(keep_half, back, jnp.zeros((), F32)).astype(BF16)
    return (grad_dec[None], grad_pre[None])


def window_kernel(
    nj, pre_hbm, thr_hbm, tiles_hbm, dec_hbm, rem_hbm, gd_ref, gp_ref,
    pre_ref, thr_ref, tiles_ref, dec_ref, rem_ref, acts_ref, flipped, back, err_ref,
    pf, csend, crecv, sx, xsend, xrecv, psend, precv, msend, mrecv,
    send_sem, recv_sem, load_sem,
):
    feat, x = lax.axis_index("feat"), lax.axis_index("layer")
    c = feat % 2
    zl, zh = feat // 2 % 2, feat // 4
    width = pf.shape[-1]
    features = pre_ref.shape[1]
    sibling = {"feat": feat + 1 - 2 * c, "layer": x}
    across = {"feat": feat, "layer": 1 - x}
    beside = {"feat": feat + 2 - 4 * zl, "layer": x}
    beyond = {"feat": feat + 4 - 8 * zh, "layer": x}
    corner = {"feat": feat + 6 - 4 * zl - 8 * zh, "layer": x}

    barrier = pltpu.get_barrier_semaphore()
    for peer in (sibling, across, beside, beyond, corner):
        pl.semaphore_signal(barrier, inc=1, device_id=peer, device_id_type=MESH)

    def cols(j):
        return slice(j * width, (j + 1) * width)

    loads = [
        pltpu.make_async_copy(src, dst, load_sem.at[i])
        for i, (src, dst) in enumerate(
            [(tiles_hbm, tiles_ref), (thr_hbm, thr_ref), (pre_hbm, pre_ref)]
            + [(dec_hbm.at[:, cols(j)], dec_ref.at[:, cols(j)]) for j in range(nj)]
            + [(rem_hbm, rem_ref)]
        )
    ]
    for load in loads:
        load.start()

    started = []

    def send(j, kind, src, dst, peer):
        copy = pltpu.make_async_remote_copy(
            src_ref=src, dst_ref=dst, send_sem=send_sem.at[j * 9 + kind],
            recv_sem=recv_sem.at[j * 9 + kind], device_id=peer, device_id_type=MESH,
        )
        copy.start()
        started.append(copy)

    def arrived(j, kind, dst):
        pltpu.make_async_remote_copy(
            src_ref=dst, dst_ref=dst, send_sem=send_sem.at[j * 9 + kind],
            recv_sem=recv_sem.at[j * 9 + kind], device_id=sibling, device_id_type=MESH,
        ).wait_recv()

    tiles_here = features // 128
    listed_count = tiles_ref.shape[0]
    shape = (listed_count * tiles_here, features)
    row_tile = lax.broadcasted_iota(jnp.int32, shape, 0) // listed_count
    col_tile = lax.broadcasted_iota(jnp.int32, shape, 1) // 128
    spread = jnp.where(row_tile == col_tile, 1.0, 0.0).astype(BF16)
    loads[0].wait()
    listed = tiles_ref[...]
    named = jnp.concatenate(
        [jnp.where(listed == feat * tiles_here + i, 1.0, 0.0) for i in range(tiles_here)], axis=0
    ).astype(BF16)
    loads[1].wait()
    loads[2].wait()
    for i in range(0, features, 256):
        part = slice(i, i + 256)
        hit = lax.dot_general(
            named, spread[:, part], (((0,), (0,)), ((), ())), preferred_element_type=F32
        )
        pre = pre_ref[:, part].astype(F32)
        keep = jnp.where(pre > thr_ref[:, part], hit, 0.0) > 0.0
        acts_ref[:, part] = jnp.where(keep, pre, 0.0).astype(BF16)

    def multiply(j):
        loads[3 + j].wait()
        part = jnp.dot(acts_ref[...], dec_ref[:, cols(j)], preferred_element_type=F32)
        pf[j] = part.reshape(pf.shape[1:])
        csend[j] = pf[j, :, :, 1 - c].astype(BF16)
        if j == 0:
            pl.semaphore_wait(barrier, 5)
        send(j, 0, csend.at[j], crecv.at[j], sibling)
        if j == 0:
            loads[3 + nj].wait()

    def add_core(j):
        arrived(j, 0, crecv.at[j])
        xsend[j] = (pf[j, :, :, c, 1 - x] + crecv[j, :, :, 1 - x].astype(F32)).astype(BF16)
        send(j, 1, xsend.at[j], xrecv.at[j], across)
        sx[j] = pf[j, :, :, c, x] + crecv[j, :, :, x].astype(F32)

    def add_layer(j):
        arrived(j, 1, xrecv.at[j])
        psend[j] = (sx[j, :, 1 - zl] + xrecv[j, :, 1 - zl].astype(F32)).astype(BF16)
        send(j, 2, psend.at[j], precv.at[j], beside)

    def add_beside(j):
        arrived(j, 2, precv.at[j])
        far = sx[j, 1 - zh, zl] + xrecv[j, 1 - zh, zl].astype(F32)
        msend[j] = (far + precv[j, 1 - zh].astype(F32)).astype(BF16)
        send(j, 3, msend.at[j], mrecv.at[j], beyond)

    def finish(j):
        near = sx[j, zh, zl] + xrecv[j, zh, zl].astype(F32) + precv[j, zh].astype(F32)
        rem = rem_ref[:, cols(j)].astype(F32)
        arrived(j, 3, mrecv.at[j])
        err_ref[j, zh, zl, c, x] = (near + mrecv[j].astype(F32) - rem).astype(BF16)
        own = err_ref.at[j, zh, zl, c, x]
        send(j, 4, own, own, beyond)
        send(j, 5, own, own, corner)
        send(j, 6, own, own, beside)

    def pass_across(j):
        arrived(j, 4, err_ref.at[j, 1 - zh, zl, c, x])
        arrived(j, 5, err_ref.at[j, 1 - zh, 1 - zl, c, x])
        arrived(j, 6, err_ref.at[j, zh, 1 - zl, c, x])
        send(j, 7, err_ref.at[j, :, :, c, x], err_ref.at[j, :, :, c, x], across)

    def pass_sibling(j):
        arrived(j, 7, err_ref.at[j, :, :, c, 1 - x])
        send(j, 8, err_ref.at[j, :, :, c], err_ref.at[j, :, :, c], sibling)

    def gradients(j):
        arrived(j, 8, err_ref.at[j, :, :, 1 - c])
        late = nj - 2
        if j < late and j % 2 == 0:
            return
        term = None
        for i in [j - 1, j] if j < late else [j]:
            err = err_ref[i].reshape(acts_ref.shape[0], width)
            gd_ref[:, cols(i)] = jnp.dot(
                flipped[...], err, preferred_element_type=F32
            ).astype(BF16)
            part = lax.dot_general(
                err, dec_ref[:, cols(i)], (((1,), (1,)), ((), ())), preferred_element_type=F32
            )
            term = part if term is None else term + part
        if j == 1:
            back[...] = term
        elif j < nj - 1:
            back[...] += term
        else:
            term = back[...] + term
            gp_ref[...] = jnp.where(acts_ref[...].astype(F32) > 0.0, term, 0.0).astype(BF16)

    def flip(j):
        if j == nj - 1:
            for i in range(0, features, 128):
                flipped[i:i + 128, :] = acts_ref[:, i:i + 128].T

    stages = [(multiply, 0), (add_core, 1), (add_layer, 3), (add_beside, 5), (finish, 7), (pass_across, 9), (pass_sibling, 11), (gradients, 12), (flip, 1)]
    for now in range(nj + max(after for _, after in stages)):
        for stage, after in stages:
            if 0 <= now - after < nj:
                stage(now - after)
    for copy in started:
        copy.wait_send()


def store_kernel(gd_ref, gp_ref, gd_hbm, gp_hbm, sem):
    rows = gd_ref.shape[0] // 4
    copies = [
        pltpu.make_async_copy(gd_ref.at[i * rows:(i + 1) * rows], gd_hbm.at[i * rows:(i + 1) * rows], sem.at[i])
        for i in range(4)
    ] + [pltpu.make_async_copy(gp_ref, gp_hbm, sem.at[4])]
    for copy in copies:
        copy.start()
    for copy in copies:
        copy.wait()


def staged(nj, pre_acts, thresholds, tile_lists, decoders, remainder):
    _, tokens, features = pre_acts.shape
    model, listed = decoders.shape[3], tile_lists.shape[2]
    width, rows = model // nj, remainder.shape[0]
    hbm = pl.BlockSpec(memory_space=pltpu.HBM)
    vmem = pl.BlockSpec(memory_space=pltpu.VMEM)
    grad_dec, grad_pre = pl.pallas_call(
        functools.partial(window_kernel, nj),
        out_shape=(
            jax.ShapeDtypeStruct((features, model), BF16),
            jax.ShapeDtypeStruct((tokens, features), BF16),
        ),
        in_specs=[hbm] * 5,
        out_specs=(vmem, vmem),
        scratch_shapes=[
            pltpu.VMEM((tokens, features), BF16),
            pltpu.VMEM((1, features), F32),
            pltpu.VMEM((listed, tokens), jnp.int32),
            pltpu.VMEM((features, model), BF16),
            pltpu.VMEM((rows, model), BF16),
            pltpu.VMEM((tokens, features), BF16),
            pltpu.VMEM((features, tokens), BF16),
            pltpu.VMEM((tokens, features), F32),
            pltpu.VMEM((nj, 2, 2, 2, 2, rows, width), BF16),
            pltpu.VMEM((nj, 2, 2, 2, 2, rows, width), F32),
            pltpu.VMEM((nj, 2, 2, 2, rows, width), BF16),
            pltpu.VMEM((nj, 2, 2, 2, rows, width), BF16),
            pltpu.VMEM((nj, 2, 2, rows, width), F32),
            pltpu.VMEM((nj, 2, 2, rows, width), BF16),
            pltpu.VMEM((nj, 2, 2, rows, width), BF16),
            pltpu.VMEM((nj, 2, rows, width), BF16),
            pltpu.VMEM((nj, 2, rows, width), BF16),
            pltpu.VMEM((nj, rows, width), BF16),
            pltpu.VMEM((nj, rows, width), BF16),
            pltpu.SemaphoreType.DMA((nj * 9,)),
            pltpu.SemaphoreType.DMA((nj * 9,)),
            pltpu.SemaphoreType.DMA((nj + 4,)),
        ],
        compiler_params=pltpu.CompilerParams(
            collective_id=0, has_side_effects=True, vmem_limit_bytes=46137344
        ),
        cost_estimate=pl.CostEstimate(
            flops=6 * tokens * features * model, bytes_accessed=12 << 20, transcendentals=0
        ),
    )(
        *(
            pltpu.with_memory_space_constraint(array, pltpu.HBM)
            for array in (
                pre_acts.reshape(tokens, features), thresholds, tile_lists.reshape(tokens, listed).T,
                decoders.reshape(features, model), remainder.reshape(rows, model),
            )
        )
    )
    grad_dec, grad_pre = pl.pallas_call(
        store_kernel,
        out_shape=(
            jax.ShapeDtypeStruct((features, model), BF16),
            jax.ShapeDtypeStruct((tokens, features), BF16),
        ),
        in_specs=[pl.BlockSpec(memory_space=pl.ANY)] * 2,
        out_specs=(hbm, hbm),
        scratch_shapes=[pltpu.SemaphoreType.DMA((5,))],
        compiler_params=pltpu.CompilerParams(vmem_limit_bytes=1 << 20),
    )(grad_dec, grad_pre)
    return grad_dec[None, None], grad_pre[None]


def solution(mesh):
    in_specs = (
        P("layer", "grp", "feat"),
        P("layer", "feat"),
        P("layer", "grp", None),
        P("layer", None, "feat", "rep"),
        P(("grp", "feat", "layer"), None, "rep"),
    )
    out_specs = (P("layer", "grp", "feat", "rep"), P("layer", "grp", ("feat", "rep")))

    def shards(*args):
        feat, layer = mesh.shape["feat"], mesh.shape["layer"]
        rows = args[4].shape[0]
        halved = feat == 8 and layer == 2 and mesh.shape["rep"] == 1
        if halved and rows % 16 == 0 and args[3].shape[1] == 1:
            return staged(8, *args)
        return general(*args)

    return jax.shard_map(shards, mesh=mesh, in_specs=in_specs, out_specs=out_specs, check_vma=False)
```
